32 devices in a mesh: section: 4 (over y, x), expert: 8 (over z, core).
Axes of the slice: x: 2, y: 2, z: 4, core: 2. Of those that a mesh axis runs over, the one named last changes fastest.
Arguments:
- layer_input: bfloat16 [4, 128, 4096], P('section', 'expert'), may hold values from -6 to 6
- w_gate: bfloat16 [4, 4096, 16384], P('section', None, 'expert'), may hold values from -0.09375 to 0.09375
- w_up: bfloat16 [4, 4096, 16384], P('section', None, 'expert'), may hold values from -0.09375 to 0.09375
- w_down: bfloat16 [4, 16384, 4096], P('section', 'expert'), may hold values from -0.1875 to 0.1875
- grad_out: bfloat16 [4, 128, 4096], P('section', 'expert'), may hold values from -1.5 to 1.5
- expert_ids: int32 [4, 128, 8], P('section', 'expert'), may hold values from 0 to 15, all different within a row; in each aligned block of 16 rows (0 to 15, 16 to 31, ..., all dimensions but the last counted through in order) at most 12 rows name the same one
- gates: bfloat16 [4, 128, 8], P('section', 'expert'), may hold values from 0.049804688 to 1
Outputs:
- grad_prev: bfloat16 [4, 128, 4096], P('section', 'expert')
- grad_w_gate: bfloat16 [4, 4096, 16384], P('section', None, 'expert')
- grad_w_up: bfloat16 [4, 4096, 16384], P('section', None, 'expert')
- grad_w_down: bfloat16 [4, 16384, 4096], P('section', 'expert')
The draws below stay inside these ranges and needn't reach their ends.
Inputs may be any that keep to these rules, and one draw needn't show every extreme that they name: `expert_ids`: each token names 8 different experts; among the 16 tokens of one index of expert (aligned blocks of rows), no expert is named more than 12 times, a bound that some block reaches.
All inputs are finite; a program needn't handle non-finite values.
Results may differ from the reference program's by a relative error of at most 0.0065.
Values may be sent and summed in bfloat16 or wider, within the bound.
No kernel may reach another device: no remote copies, remote signals or barrier semaphores. Data moves between devices by JAX's collectives and lax.ppermute only.
A program may use at most 192 MiB of HBM per device.

```python
import math
import jax
import jax.numpy as jnp
import numpy as np
from jax import lax

D = 4096
HID = 1024
TOPK = 8
EXPERTS = 16
TOK_DEV = 16
SECTIONS = 4
TOKENS = 128
CAP = 12
SLOTS = 96
HBLOCK = 1024
N_EXPERT = 8


def block_levels(rng, shape, pieces, smallest, top_value):
    loudness, own = 1.0, jax.random.fold_in(rng, 6)
    for axis_at, blocks in pieces:
        steps = jnp.exp(jax.random.uniform(jax.random.fold_in(own, axis_at), (blocks,), jnp.float32, smallest / len(pieces), top_value / len(pieces)))
        loudness = loudness * jnp.repeat(steps, shape[axis_at] // blocks).reshape([-1 if axis == axis_at else 1 for axis in range(len(shape))])
    return loudness


def routed_block(stream_key, own, number, rows, number_of, top, most, slope):
    sequence = jax.random.permutation(stream_key, number_of)
    crowded, ordinary = shares(number_of, rows * top, most, slope, True), shares(number_of, rows * top, most, slope, False)
    places = jnp.arange(number_of)

    def named(sizes, turn):
        used = int((sizes > 0).sum())
        fixed = max(1, used // 4)
        passed = fixed + (places - fixed + turn * (used - fixed)) % max(1, number_of - fixed)
        return jnp.zeros((number_of,), jnp.int32).at[sequence[jnp.where(places < fixed, places, passed)]].set(jnp.asarray(sizes, jnp.int32))

    sizes = jnp.where(number % 4 == 0, named(crowded, number // 4), named(ordinary, number - number // 4 - 1))
    mixed = jax.random.permutation(jax.random.fold_in(own, 3), number_of)
    donor, taker = mixed[0:number_of // 2 * 2:2], mixed[1:number_of // 2 * 2:2]
    margin = jnp.minimum(sizes[donor] - 1, most - sizes[taker]) // 2
    margin = jnp.where((donor == sequence[0]) | (taker == sequence[0]) | (sizes[taker] == 0), 0, jnp.maximum(margin, 0))
    passed = jax.random.randint(jax.random.fold_in(own, 4), (number_of // 2,), 0, 1 << 20) % (margin + 1)
    sizes = sizes.at[donor].add(-passed).at[taker].add(passed)
    items = jnp.searchsorted(jnp.cumsum(sizes), jnp.arange(rows * top), side="right").astype(jnp.int32)
    grid = items.reshape(top, rows).T
    grid = grid[jax.random.permutation(jax.random.fold_in(own, 1), rows)]
    turn = jax.random.randint(jax.random.fold_in(own, 2), (rows, 1), 0, top)
    return jnp.take_along_axis(grid, (jnp.arange(top)[None, :] + turn) % top, axis=1)


def shares(count, total, bound, skew, full):
    weights = [(1 << 20) // math.isqrt(grade ** skew) + 1 for grade in range(1, count + 1)]
    largest = bound if full else min(bound, max(-(-total // count), total * weights[0] // sum(weights)))
    least = 1 if total - largest >= count - 1 else 0
    holding, spare = [largest] + [least] * (count - 1), total - largest - least * (count - 1)
    while spare > 0:
        movable = [i for i in range(1, count) if holding[i] < largest] or [i for i in range(1, count) if holding[i] < bound]
        whole, left = sum([weights[i] for i in movable]), spare
        for i in movable:
            more = min(bound - holding[i], max(1, left * weights[i] // whole), spare)
            holding[i] = holding[i] + more
            spare = spare - more
    return np.array(holding)


def gaussian(key, dims, deviation, reach, cuts=(), dtype=jnp.bfloat16):
    drawn = deviation * jax.random.normal(key, dims, jnp.float32)
    if cuts:
        drawn = drawn * block_levels(key, dims, cuts, -0.22, 0.18)
    return jnp.clip(drawn, -reach, reach).astype(dtype)


def setup_inputs(seed: int = 0) -> dict:
    seeds = jax.random.split(jax.random.key(seed), 8)
    layer_input = gaussian(seeds[0], (SECTIONS, TOKENS, D), 1.0, 6.0, ((0, 4), (1, 8)))
    w_gate = gaussian(seeds[1], (SECTIONS, D, EXPERTS * HID), D ** -0.5, 0.09375, ((0, 4), (2, 8)))
    w_up = gaussian(seeds[2], (SECTIONS, D, EXPERTS * HID), D ** -0.5, 0.09375, ((0, 4), (2, 8)))
    w_down = gaussian(seeds[3], (SECTIONS, EXPERTS * HID, D), HID ** -0.5, 0.1875, ((0, 4), (1, 8)))
    grad_out = gaussian(seeds[4], (SECTIONS, TOKENS, D), 0.25, 1.5, ((0, 4), (1, 8)))
    expert_ids_keys = jax.random.split(jax.random.fold_in(seeds[5], 1), SECTIONS * TOKENS // TOK_DEV)
    expert_ids_turns = jax.random.permutation(jax.random.fold_in(seeds[5], 3), SECTIONS * TOKENS // TOK_DEV)
    expert_ids = jax.vmap(lambda own, number: routed_block(jax.random.fold_in(seeds[5], 2), own, number, TOK_DEV, EXPERTS, TOPK, CAP, 2))(expert_ids_keys, expert_ids_turns).reshape((SECTIONS, TOKENS, TOPK))
    gates = jnp.clip(0.049804688 + 0.9501953 * jax.random.uniform(seeds[6], (SECTIONS, TOKENS, TOPK), jnp.float32) ** block_levels(seeds[6], (SECTIONS, TOKENS, TOPK), ((0, 4), (1, 8)), -0.2, 0.2), 0.049804688, 1.0).astype(jnp.bfloat16)
    return {"layer_input": layer_input, "w_gate": w_gate, "w_up": w_up, "w_down": w_down, "grad_out": grad_out, "expert_ids": expert_ids, "gates": gates}


def local_slots(expert_ids, experts):
    picked = (expert_ids[..., None] == lax.iota(jnp.int32, experts)).astype(jnp.int32).sum(axis=-2)
    before = jnp.cumsum(picked, axis=-2) - picked
    return jnp.take_along_axis(before, expert_ids, axis=-1).astype(jnp.int32)


def contract(left, right, left_dim, right_dim):
    return lax.dot_general(left, right, (((left_dim,), (right_dim,)), ((), ())), preferred_element_type=jnp.float32)


def expert_grads(inputs, cotangent, w_gate, w_up, w_down):
    gate_pre = jnp.dot(inputs, w_gate, preferred_element_type=jnp.float32)
    up_pre = jnp.dot(inputs, w_up, preferred_element_type=jnp.float32)
    sigmoid = jax.nn.sigmoid(gate_pre)
    active = gate_pre * sigmoid
    hidden = (active * up_pre).astype(jnp.bfloat16)
    hidden_grad = contract(cotangent, w_down, 1, 1)
    gate_grad = (hidden_grad * up_pre * sigmoid * (1.0 + gate_pre * (1.0 - sigmoid))).astype(jnp.bfloat16)
    up_grad = (hidden_grad * active).astype(jnp.bfloat16)
    total = jnp.zeros((inputs.shape[0], inputs.shape[1]), jnp.float32)
    for start in range(0, HID, HBLOCK):
        part = (contract(gate_grad[:, start:start + HBLOCK], w_gate[:, start:start + HBLOCK], 1, 1)
                + contract(up_grad[:, start:start + HBLOCK], w_up[:, start:start + HBLOCK], 1, 1)).astype(jnp.bfloat16)
        total = total + lax.optimization_barrier(part).astype(jnp.float32)
    return total, contract(inputs, gate_grad, 0, 0), contract(inputs, up_grad, 0, 0), contract(hidden, cotangent, 0, 0)


def reference(layer_input, w_gate, w_up, w_down, grad_out, expert_ids, gates):
    inputs_all, gate_all, up_all, down_all = [], [], [], []
    for section_index in range(SECTIONS):
        picks = expert_ids[section_index].reshape(N_EXPERT, TOK_DEV, TOPK)
        slot_index = local_slots(picks, EXPERTS)
        source = lax.iota(jnp.int32, N_EXPERT)[:, None, None]
        target = (picks * SLOTS + source * CAP + slot_index).reshape(-1).astype(jnp.int32)
        scaled = (gates[section_index].astype(jnp.float32)[:, :, None] * grad_out[section_index].astype(jnp.float32)[:, None, :]).astype(jnp.bfloat16).reshape(-1, D)
        copies = jnp.broadcast_to(layer_input[section_index][:, None, :], (TOKENS, TOPK, D)).reshape(-1, D)
        dispatched = jnp.zeros((EXPERTS * SLOTS, D), jnp.bfloat16).at[target].set(scaled).reshape(EXPERTS, SLOTS, D)
        rows_in = jnp.zeros((EXPERTS * SLOTS, D), jnp.bfloat16).at[target].set(copies).reshape(EXPERTS, SLOTS, D)
        gate_w = w_gate[section_index].reshape(D, EXPERTS, HID).transpose(1, 0, 2)
        up_w = w_up[section_index].reshape(D, EXPERTS, HID).transpose(1, 0, 2)
        down_w = w_down[section_index].reshape(EXPERTS, HID, D)
        rows_grad, gate_grad, up_grad, down_grad = lax.map(
            lambda items: expert_grads(*items),
            (rows_in, dispatched, gate_w, up_w, down_w))
        gathered = rows_grad.reshape(-1, D)[target].reshape(TOKENS, TOPK, D)
        inputs_all.append(jnp.sum(gathered, axis=1).astype(jnp.bfloat16))
        gate_all.append(gate_grad.astype(jnp.bfloat16).transpose(1, 0, 2).reshape(D, EXPERTS * HID))
        up_all.append(up_grad.astype(jnp.bfloat16).transpose(1, 0, 2).reshape(D, EXPERTS * HID))
        down_all.append(down_grad.astype(jnp.bfloat16).reshape(EXPERTS * HID, D))
    grad_prev = jnp.roll(jnp.stack(inputs_all), -1, axis=0)
    return grad_prev, jnp.stack(gate_all), jnp.stack(up_all), jnp.stack(down_all)
```

```python
import functools

import jax
import jax.numpy as jnp
from jax import lax
from jax.experimental import pallas as pl
from jax.experimental.pallas import tpu as pltpu
from jax.sharding import PartitionSpec as P

EXPERTS = 16
LANES = 128
BF16, F32 = jnp.bfloat16, jnp.float32
MIB = 1 << 20


def contract(left, right, left_dim, right_dim):
    return lax.dot_general(
        left, right, (((left_dim,), (right_dim,)), ((), ())), preferred_element_type=F32
    )


def swap(block, bits):
    devices = lax.axis_size("expert")
    return lax.ppermute(block, "expert", [(i, i ^ bits) for i in range(devices)])


def across(block):
    devices = lax.axis_size("expert")
    found = {0: block}
    bits = devices // 2
    while bits > 1:
        found |= {mask | bits: swap(part, bits) for mask, part in found.items()}
        bits //= 2
    return found


def gather(block):
    near = across(block)
    masks = sorted(near)
    return [near[m] for m in masks] + [swap(near[m], 1) for m in masks]


def params(limit):
    return pltpu.CompilerParams(vmem_limit_bytes=limit * MIB)


def cost(flops, moved):
    return pl.CostEstimate(flops=flops, bytes_accessed=moved, transcendentals=0)


def joined(refs):
    return jnp.concatenate([r[...] for r in refs], axis=0) if len(refs) > 1 else refs[0][...]


def pre_kernel(count, *refs):
    pieces, (gate_ref, up_ref, x_ref, a_ref, b_ref) = refs[:count], refs[count:]

    @pl.when(pl.program_id(0) == 0)
    def _():
        a_ref[...] = jnp.zeros_like(a_ref)
        b_ref[...] = jnp.zeros_like(b_ref)

    x = joined(pieces)
    x_ref[...] = x
    a_ref[...] += jnp.dot(x, gate_ref[...], preferred_element_type=F32)
    b_ref[...] += jnp.dot(x, up_ref[...], preferred_element_type=F32)


def pre(pieces, w_gate, w_up):
    width, columns = w_gate.shape
    tokens = sum(p.shape[0] for p in pieces)
    depth = min(512, width)
    return pl.pallas_call(
        functools.partial(pre_kernel, len(pieces)),
        grid=(width // depth,),
        in_specs=[pl.BlockSpec((p.shape[0], depth), lambda i: (0, i)) for p in pieces]
        + [pl.BlockSpec((depth, columns), lambda i: (i, 0))] * 2,
        out_specs=[pl.BlockSpec((tokens, depth), lambda i: (0, i))]
        + [pl.BlockSpec((tokens, columns), lambda i: (0, 0))] * 2,
        out_shape=[jax.ShapeDtypeStruct((tokens, width), BF16)]
        + [jax.ShapeDtypeStruct((tokens, columns), F32)] * 2,
        compiler_params=params(40),
        cost_estimate=cost(4 * tokens * width * columns, 4 * width * columns),
    )(*pieces, w_gate, w_up)


def mid_kernel(count, width, per_expert, first_ref, *refs):
    pieces, refs = refs[:count], refs[count:]
    down_ref, a_ref, b_ref, c_ref, gg_ref, ug_ref, h_ref = refs
    step = pl.program_id(0)

    @pl.when(step == 0)
    def _():
        c_ref[...] = joined([p.at[:, :width] for p in pieces])

    gates = joined([p.at[:, width:] for p in pieces]).astype(F32)
    lane = lax.broadcasted_iota(jnp.int32, gates.shape, 1)
    own = first_ref[0] + step // per_expert
    weight = jnp.sum(jnp.where(lane == own, gates, 0.0), axis=1, keepdims=True)
    hidden_grad = weight * contract(c_ref[...], down_ref[...], 1, 1)
    a, b = a_ref[...], b_ref[...]
    g = jax.nn.sigmoid(a)
    active = a * g
    h_ref[...] = (weight * (active * b)).astype(BF16)
    ug_ref[...] = (hidden_grad * active).astype(BF16)
    gg_ref[...] = (hidden_grad * b * g * (1.0 + a * (1.0 - g))).astype(BF16)


def mid(first, pieces, w_down, a, b, experts):
    columns, width = w_down.shape
    tokens = a.shape[0]
    block = min(256, columns // experts)
    narrow = pl.BlockSpec((tokens, block), lambda i: (0, i))
    return pl.pallas_call(
        functools.partial(mid_kernel, len(pieces), width, columns // experts // block),
        grid=(columns // block,),
        in_specs=[pl.BlockSpec(memory_space=pltpu.SMEM)]
        + [pl.BlockSpec(p.shape, lambda i: (0, 0)) for p in pieces]
        + [pl.BlockSpec((block, width), lambda i: (i, 0)), narrow, narrow],
        out_specs=[pl.BlockSpec((tokens, width), lambda i: (0, 0))] + [narrow] * 3,
        out_shape=[jax.ShapeDtypeStruct((tokens, width), BF16)]
        + [jax.ShapeDtypeStruct((tokens, columns), BF16)] * 3,
        compiler_params=params(40),
        cost_estimate=cost(2 * tokens * width * columns, 2 * width * columns),
    )(first, *pieces, w_down, a, b)


def row_kernel(gg_ref, ug_ref, gate_ref, up_ref, far_ref, near_ref):
    rows = contract(gg_ref[...], gate_ref[...], 1, 1) + contract(ug_ref[...], up_ref[...], 1, 1)
    half = near_ref.shape[0]
    near_ref[...] = rows[:half].astype(BF16)
    far_ref[...] = rows[half:].astype(BF16)


def row(gg, ug, w_gate, w_up, part, parts):
    tokens, columns = gg.shape
    width = w_gate.shape[0] // parts
    block = min(512, width)
    base = part * (width // block)
    whole = pl.BlockSpec((tokens, columns), lambda i: (0, 0))
    return pl.pallas_call(
        row_kernel,
        grid=(width // block,),
        in_specs=[whole, whole] + [pl.BlockSpec((block, columns), lambda i: (base + i, 0))] * 2,
        out_specs=[pl.BlockSpec((tokens // 2, block), lambda i: (0, i))] * 2,
        out_shape=[jax.ShapeDtypeStruct((tokens // 2, width), BF16)] * 2,
        compiler_params=params(40),
        cost_estimate=cost(4 * tokens * width * columns, 4 * width * columns),
    )(gg, ug, w_gate, w_up)


def grads_kernel(x_ref, gg_ref, ug_ref, h_ref, c_ref, gate_ref, up_ref, down_ref):
    gate_ref[...] = contract(x_ref[...], gg_ref[...], 0, 0).astype(BF16)
    up_ref[...] = contract(x_ref[...], ug_ref[...], 0, 0).astype(BF16)
    down_ref[...] = contract(h_ref[...], c_ref[...], 0, 0).astype(BF16)


def grads(x, gg, ug, h, c):
    tokens, width = x.shape
    columns = gg.shape[1]
    steps = max(1, min(8, columns // LANES))
    high, low = width // steps, columns // steps
    tall = pl.BlockSpec((high, columns), lambda i: (i, 0))
    return pl.pallas_call(
        grads_kernel,
        grid=(steps,),
        in_specs=[
            pl.BlockSpec((tokens, high), lambda i: (0, i)),
            pl.BlockSpec((tokens, columns), lambda i: (0, 0)),
            pl.BlockSpec((tokens, columns), lambda i: (0, 0)),
            pl.BlockSpec((tokens, low), lambda i: (0, i)),
            pl.BlockSpec((tokens, width), lambda i: (0, 0)),
        ],
        out_specs=[tall, tall, pl.BlockSpec((low, width), lambda i: (i, 0))],
        out_shape=[jax.ShapeDtypeStruct((width, columns), BF16)] * 2
        + [jax.ShapeDtypeStruct((columns, width), BF16)],
        compiler_params=params(48),
        cost_estimate=cost(6 * tokens * width * columns, 6 * width * columns),
    )(x, gg, ug, h, c)


def deliver(near, far):
    devices, sections = lax.axis_size("expert"), lax.axis_size("section")
    mine = (near.astype(F32) + swap(far, 1).astype(F32)).astype(BF16)
    mine = mine.reshape(devices // 2, -1, near.shape[1])
    total = None
    for m in range(devices // 2):
        route = [
            (s * devices + i, (s - 1) % sections * devices + (i ^ (2 * m)))
            for s in range(sections)
            for i in range(devices)
        ]
        part = lax.ppermute(mine[m], ("section", "expert"), route).astype(F32)
        total = part if total is None else total + part
    return total.astype(BF16)


def body(layer_input, w_gate, w_up, w_down, grad_out, expert_ids, gates):
    devices = lax.axis_size("expert")
    experts = max(1, EXPERTS // devices)
    split = max(1, devices // EXPERTS)
    first = (lax.axis_index("expert") * experts // split).astype(jnp.int32).reshape(1)
    w_gate, w_up, w_down = w_gate[0], w_up[0], w_down[0]
    chosen = expert_ids[0][:, :, None] == lax.iota(jnp.int32, LANES)
    weight = jnp.sum(jnp.where(chosen, gates[0][:, :, None].astype(F32), 0.0), axis=1)
    message = jnp.concatenate([grad_out[0], weight.astype(BF16)], axis=1)
    inputs, cotangents = gather(layer_input[0]), gather(message)
    if devices > 8:
        inputs, cotangents = [jnp.concatenate(inputs)], [jnp.concatenate(cotangents)]
    x, a, b = pre(inputs, w_gate, w_up)
    c, gg, ug, h = mid(first, cotangents, w_down, a, b, experts)
    parts = 2
    rows = [row(gg, ug, w_gate, w_up, part, parts) for part in range(parts)]
    gate_grad, up_grad, down_grad = grads(x, gg, ug, h, c)
    grad_prev = jnp.concatenate([deliver(near, far) for far, near in rows], axis=1)
    return grad_prev[None], gate_grad[None], up_grad[None], down_grad[None]


def solution(mesh):
    tokens, columns = P("section", "expert", None), P("section", None, "expert")
    return jax.shard_map(
        body,
        mesh=mesh,
        in_specs=(tokens, columns, columns, tokens, tokens, tokens, tokens),
        out_specs=(tokens, columns, columns, tokens),
        check_vma=False,
    )
```

```python
import functools

import jax
import jax.numpy as jnp
from jax import lax
from jax.experimental import pallas as pl
from jax.experimental.pallas import tpu as pltpu
from jax.sharding import PartitionSpec as P

EXPERTS = 16
LANES = 128
SLOTS = 5
BF16, F32 = jnp.bfloat16, jnp.float32
MIB = 1 << 20
WHOLE = pl.BlockSpec(memory_space=pltpu.VMEM)


def contract(left, right, left_dim, right_dim):
    return lax.dot_general(
        left, right, (((left_dim,), (right_dim,)), ((), ())), preferred_element_type=F32
    )


def swap(block, bits):
    devices = lax.axis_size("expert")
    return lax.ppermute(block, "expert", [(i, i ^ bits) for i in range(devices)])


def across(block, token):
    devices = lax.axis_size("expert")
    found = {0: block}
    bits = devices // 2
    while bits > 1:
        found |= {mask | bits: swap(part, bits) for mask, part in found.items()}
        if token is not None and bits == devices // 2:
            found[bits], token = lax.optimization_barrier((found[bits], token))
        bits //= 2
    return found, token


def gather(block, token=None):
    near, token = across(block, token)
    masks = sorted(near)
    return [near[m] for m in masks] + [swap(near[m], 1) for m in masks], token


def in_hbm(array):
    return pltpu.with_memory_space_constraint(array, pltpu.HBM)


def kernel_call(kernel, operands, outs, limit, flops, moved, **more):
    specs = more.pop("in_specs", [WHOLE] * len(operands))
    return pl.pallas_call(
        kernel,
        in_specs=specs,
        out_specs=more.pop("out_specs", [WHOLE] * len(outs)),
        out_shape=outs,
        compiler_params=pltpu.CompilerParams(vmem_limit_bytes=limit * MIB),
        cost_estimate=pl.CostEstimate(flops=flops, bytes_accessed=moved, transcendentals=0),
        **more,
    )(*operands)


def joined(refs, columns):
    parts = [r[:, columns] for r in refs]
    return jnp.concatenate(parts, axis=0) if len(parts) > 1 else parts[0]


def fetch_kernel(pieces, from_ref, to_ref, token_ref, sems):
    token_ref[...] = jnp.zeros_like(token_ref)
    rows = from_ref.shape[0] // pieces
    parts = [pl.ds(i * rows, rows) for i in range(pieces)]
    copies = [
        pltpu.make_async_copy(from_ref.at[part], to_ref.at[part], sems.at[i])
        for i, part in enumerate(parts)
    ]
    for copy in copies:
        copy.start()
    for copy in copies:
        copy.wait()


def fetch(weights, pieces=4):
    return kernel_call(
        functools.partial(fetch_kernel, pieces),
        [in_hbm(weights)],
        [pltpu.VMEM(weights.shape, weights.dtype), jax.ShapeDtypeStruct((8, LANES), F32)],
        1,
        0,
        2 * weights.size,
        in_specs=[pl.BlockSpec(memory_space=pltpu.HBM)],
        scratch_shapes=[pltpu.SemaphoreType.DMA((pieces,))],
    )


def pre_kernel(count, *refs):
    pieces, refs = refs[:count], refs[count + 1 :]
    gate_ref, up_ref, at_ref, bt_ref, xt_ref, a_ref, b_ref = refs
    width = gate_ref.shape[0]
    depth = min(512, width)
    for start in range(0, width, depth):
        rows = pl.ds(start, depth)
        x = joined(pieces, rows)
        xt_ref[rows, :] = x.T
        a = jnp.dot(x, gate_ref[rows, :], preferred_element_type=F32)
        b = jnp.dot(x, up_ref[rows, :], preferred_element_type=F32)
        if start:
            a, b = a_ref[...] + a, b_ref[...] + b
        a_ref[...], b_ref[...] = a, b
    at_ref[...], bt_ref[...] = a_ref[...].T, b_ref[...].T


def pre(pieces, token, w_gate, w_up):
    width, columns = w_gate.shape
    tokens = sum(p.shape[0] for p in pieces)
    count = len(pieces)
    return kernel_call(
        functools.partial(pre_kernel, count),
        [*pieces, token, w_gate, w_up],
        [jax.ShapeDtypeStruct((columns, tokens), F32)] * 2
        + [jax.ShapeDtypeStruct((width, tokens), BF16)],
        6,
        4 * tokens * width * columns,
        2 * tokens * width,
        scratch_shapes=[pltpu.VMEM((tokens, columns), F32)] * 2,
    )


def core_kernel(count, experts, split, *refs):
    pieces, refs = refs[:count], refs[count:]
    at_ref, bt_ref, down_ref, gate_ref, up_ref = refs[:5]
    c_ref, ggt_ref, ugt_ref, ht_ref, near_ref, far_ref = refs[5:11]
    downs, gate_slots, up_slots, down_sems, gate_sems, up_sems = refs[11:]
    columns, width = down_ref.shape
    each, block, depth = columns // experts, downs.shape[1], gate_slots.shape[1]
    steps, turns, half = columns // block, width // depth, near_ref.shape[0]
    ahead = SLOTS - 1

    def arrivals(ref, slots, sems, step):
        rows = pl.ds(pl.multiple_of(step * slots.shape[1], slots.shape[1]), slots.shape[1])
        slot = lax.rem(step, SLOTS)
        return pltpu.make_async_copy(ref.at[rows], slots.at[slot], sems.at[slot])

    def down(step):
        return arrivals(down_ref, downs, down_sems, step)

    def gate(turn):
        return arrivals(gate_ref, gate_slots, gate_sems, turn)

    def up(turn):
        return arrivals(up_ref, up_slots, up_sems, turn)

    def start_pair(turn):
        gate(turn).start()
        up(turn).start()

    for step in range(min(ahead, steps)):
        down(jnp.int32(step)).start()
    for turn in range(min(ahead, turns) - min(ahead, steps)):
        start_pair(jnp.int32(turn))
    at = 0
    for piece in pieces:
        c_ref[pl.ds(at, piece.shape[0]), :] = piece[:, :width]
        at += piece.shape[0]
    gates = joined(pieces, slice(width, None)).astype(F32).T
    line = lax.broadcasted_iota(jnp.int32, gates.shape, 0)
    first = lax.axis_index("expert") * experts // split
    begun = max(0, min(ahead, turns) - min(ahead, steps))

    def units(step, carry):
        down(step).wait()
        last = step + ahead - steps

        @pl.when(last < 0)
        def _():
            down(step + ahead).start()

        @pl.when((last >= begun) & (last < min(ahead, turns)))
        def _():
            start_pair(last)

        rows = pl.ds(pl.multiple_of(step * block, block), block)
        own = line == first + step * block // each
        weight = jnp.sum(jnp.where(own, gates, 0.0), axis=0, keepdims=True)
        hidden_grad = weight * contract(downs[lax.rem(step, SLOTS)], c_ref[...], 1, 1)
        a, b = at_ref[rows, :], bt_ref[rows, :]
        g = jax.nn.sigmoid(a)
        active = a * g
        ht_ref[rows, :] = (weight * (active * b)).astype(BF16)
        ugt_ref[rows, :] = (hidden_grad * active).astype(BF16)
        ggt_ref[rows, :] = (hidden_grad * b * g * (1.0 + a * (1.0 - g))).astype(BF16)
        return carry

    def rows_out(turn, carry):
        gate(turn).wait()
        up(turn).wait()

        @pl.when(turn + ahead < turns)
        def _():
            start_pair(turn + ahead)

        rows, slot = pl.ds(pl.multiple_of(turn * depth, depth), depth), lax.rem(turn, SLOTS)
        total = jnp.dot(gate_slots[slot], ggt_ref[...], preferred_element_type=F32)
        total += jnp.dot(up_slots[slot], ugt_ref[...], preferred_element_type=F32)
        total = total.T.astype(BF16)
        near_ref[:, rows] = total[:half]
        far_ref[:, rows] = total[half:]
        return carry

    lax.fori_loop(0, steps, units, 0)
    lax.fori_loop(0, turns, rows_out, 0)


def core(pieces, at, bt, w_down, w_gate, w_up, experts, split):
    columns, width = w_down.shape
    tokens = at.shape[1]
    block, depth = min(256, columns // experts), min(512, width)
    return kernel_call(
        functools.partial(core_kernel, len(pieces), experts, split),
        [*pieces, at, bt, in_hbm(w_down), in_hbm(w_gate), in_hbm(w_up)],
        [jax.ShapeDtypeStruct((tokens, width), BF16)]
        + [jax.ShapeDtypeStruct((columns, tokens), BF16)] * 3
        + [jax.ShapeDtypeStruct((tokens // 2, width), BF16)] * 2,
        40,
        12 * tokens * width * columns,
        6 * width * columns,
        in_specs=[WHOLE] * (len(pieces) + 2) + [pl.BlockSpec(memory_space=pltpu.HBM)] * 3,
        scratch_shapes=[pltpu.VMEM((SLOTS, block, width), BF16)]
        + [pltpu.VMEM((SLOTS, depth, columns), BF16)] * 2
        + [pltpu.SemaphoreType.DMA((SLOTS,))] * 3,
    )


def grads_kernel(form, *refs):
    count = len(form)
    operands, outs = refs[: 2 * count], refs[2 * count + 1 : 3 * count + 1]
    token_ref, slots, sems = refs[3 * count + 1 :]
    token_ref[...] = refs[2 * count][...]
    flying, turn = {}, 0
    for k, right_dim in enumerate(form):
        left, right, out = operands[2 * k], operands[2 * k + 1], outs[k]
        rows, columns = out.shape
        wide = slots.shape[2]
        block = slots.shape[1] * wide // columns
        for start in range(0, rows, slots.shape[1]):
            at = pl.ds(start, slots.shape[1])
            for side in range(0, columns, wide):
                slot = turn % SLOTS
                turn += 1
                if slot in flying:
                    flying.pop(slot).wait()
                part = pl.ds(side, wide)
                rhs = right[:, part] if right_dim == 0 else right[part, :]
                slots[slot] = contract(left[at, :], rhs, 1, right_dim).astype(BF16)
                flying[slot] = pltpu.make_async_copy(slots.at[slot], out.at[at, part], sems.at[slot])
                flying[slot].start()
    for copy in flying.values():
        copy.wait()


def grads(token, *products):
    operands, outs, form, flops = [], [], [], 0
    for left, right, right_dim in products:
        operands += [left, right]
        form.append(right_dim)
        outs.append(jax.ShapeDtypeStruct((left.shape[0], right.shape[1 - right_dim]), BF16))
        flops += 4 * left.size * right.shape[1 - right_dim]
    wide = min(2048, min(o.shape[1] for o in outs))
    high = min(512, min(o.shape[0] for o in outs))
    moved = sum(2 * o.size for o in outs)
    return kernel_call(
        functools.partial(grads_kernel, tuple(form)),
        [*operands, token],
        [*outs, jax.ShapeDtypeStruct(token.shape, token.dtype)],
        20,
        flops,
        moved,
        out_specs=[pl.BlockSpec(memory_space=pltpu.HBM)] * len(outs) + [WHOLE],
        scratch_shapes=[pltpu.VMEM((SLOTS, high, wide), BF16), pltpu.SemaphoreType.DMA((SLOTS,))],
    )


def hand_on(mine, mask):
    devices, sections = lax.axis_size("expert"), lax.axis_size("section")
    route = [
        (s * devices + i, (s - 1) % sections * devices + (i ^ (2 * mask)))
        for s in range(sections)
        for i in range(devices)
    ]
    return lax.ppermute(mine, ("section", "expert"), route)


def body(layer_input, w_gate, w_up, w_down, grad_out, expert_ids, gates):
    devices = lax.axis_size("expert")
    experts = max(1, EXPERTS // devices)
    split = max(1, devices // EXPERTS)
    w_gate, w_up, w_down = w_gate[0], w_up[0], w_down[0]
    chosen = expert_ids[0][:, :, None] == lax.iota(jnp.int32, LANES)
    weight = jnp.sum(jnp.where(chosen, gates[0][:, :, None].astype(F32), 0.0), axis=1)
    message = jnp.concatenate([grad_out[0], weight.astype(BF16)], axis=1)
    (gate_near, token), (up_near, _) = fetch(w_gate), fetch(w_up)
    inputs, token = gather(layer_input[0], token)
    cotangents, _ = gather(message)
    if devices > 8:
        inputs, cotangents = [jnp.concatenate(inputs)], [jnp.concatenate(cotangents)]
    at, bt, xt = pre(inputs, token, gate_near, up_near)
    c, ggt, ugt, ht, near, far = core(cotangents, at, bt, w_down, w_gate, w_up, experts, split)
    gate_grad, token = grads(token, (xt, ggt, 1))
    mine = (near.astype(F32) + swap(far, 1).astype(F32)).astype(BF16)
    chips = devices // 2
    mine = jnp.split(mine, chips)
    far_first = sorted(range(chips), reverse=True)
    early = [m for m in far_first if m >= chips - chips // 4 or m < chips // 4]
    late = [m for m in far_first if m not in early]
    mine, token = lax.optimization_barrier((mine, token))
    arrived = [hand_on(mine[m], m) for m in early]
    up_grad, token = grads(token, (xt, ugt, 1))
    mine, token = lax.optimization_barrier((mine, token))
    arrived += [hand_on(mine[m], m) for m in late]
    down_grad, _ = grads(token, (ht, c, 0))
    grad_prev = functools.reduce(jnp.add, [part.astype(F32) for part in arrived]).astype(BF16)
    return grad_prev[None], gate_grad[None], up_grad[None], down_grad[None]


def solution(mesh):
    tokens, columns = P("section", "expert", None), P("section", None, "expert")
    return jax.shard_map(
        body,
        mesh=mesh,
        in_specs=(tokens, columns, columns, tokens, tokens, tokens, tokens),
        out_specs=(tokens, columns, columns, tokens),
        check_vma=False,
    )
```

```python
import functools

import jax
import jax.numpy as jnp
from jax import lax
from jax.experimental import pallas as pl
from jax.experimental.pallas import tpu as pltpu
from jax.sharding import PartitionSpec as P

EXPERTS = 16
LANES = 128
SLOTS = 4
STREAM = 4
BF16, F32 = jnp.bfloat16, jnp.float32
MIB = 1 << 20
WHOLE = pl.BlockSpec(memory_space=pltpu.VMEM)


def contract(left, right, left_dim, right_dim):
    return lax.dot_general(
        left, right, (((left_dim,), (right_dim,)), ((), ())), preferred_element_type=F32
    )


def swap(block, bits):
    devices = lax.axis_size("expert")
    return lax.ppermute(block, "expert", [(i, i ^ bits) for i in range(devices)])


def gather(block, ahead, after):
    near = {0: block}
    chips = lax.axis_size("expert") // 2
    bits = chips
    while bits > 1:
        near |= {mask | bits: swap(part, bits) for mask, part in near.items()}
        if ahead is not None and bits == chips:
            near[bits], ahead = lax.optimization_barrier((near[bits], ahead))
        bits //= 2
    parts = [near[mask] for mask in sorted(near)]
    other = [swap(part, 1) for part in parts[:-1]]
    if after is not None:
        parts[-1], after = lax.optimization_barrier((parts[-1], after))
    return parts + other + [swap(parts[-1], 1)], ahead, after


def in_hbm(array):
    return pltpu.with_memory_space_constraint(array, pltpu.HBM)


def kernel_call(kernel, operands, outs, limit, flops, moved, **more):
    specs = more.pop("in_specs", [WHOLE] * len(operands))
    return pl.pallas_call(
        kernel,
        in_specs=specs,
        out_specs=more.pop("out_specs", [WHOLE] * len(outs)),
        out_shape=outs,
        compiler_params=pltpu.CompilerParams(vmem_limit_bytes=limit * MIB),
        cost_estimate=pl.CostEstimate(flops=flops, bytes_accessed=moved, transcendentals=0),
        **more,
    )(*operands)


def joined(refs, columns):
    parts = [r[:, columns] for r in refs]
    return jnp.concatenate(parts, axis=0) if len(parts) > 1 else parts[0]


def message_kernel(grad_ref, ids_ref, gates_ref, out_ref, token_ref):
    token_ref[...] = jnp.zeros_like(token_ref)
    rows, width = grad_ref.shape
    out_ref[:, :width] = grad_ref[...]
    lane = lax.broadcasted_iota(jnp.int32, (rows, LANES), 1)
    weight = jnp.zeros((rows, LANES), F32)
    for k in range(ids_ref.shape[1]):
        own = ids_ref[:, k : k + 1] == lane
        weight += jnp.where(own, gates_ref[:, k : k + 1].astype(F32), 0.0)
    out_ref[:, width:] = weight.astype(BF16)


def message_of(grad_out, ids, gates, beside):
    rows, width = grad_out.shape
    return kernel_call(
        message_kernel,
        [grad_out, ids, gates],
        [jax.ShapeDtypeStruct((rows, width + LANES), BF16), jax.ShapeDtypeStruct((8, LANES), F32)],
        4,
        beside,
        4 * rows * width,
    )


def pre_kernel(count, *refs):
    pieces, refs = refs[:count], refs[count + 1 :]
    gate_ref, up_ref, at_ref, bt_ref, xt_ref, token_ref, a_ref, b_ref = refs
    token_ref[...] = jnp.zeros_like(token_ref)
    width = gate_ref.shape[0]
    depth = min(512, width)
    for start in range(0, width, depth):
        rows = pl.ds(start, depth)
        x = joined(pieces, rows)
        xt_ref[rows, :] = x.T
        a = jnp.dot(x, gate_ref[rows, :], preferred_element_type=F32)
        b = jnp.dot(x, up_ref[rows, :], preferred_element_type=F32)
        if start:
            a, b = a_ref[...] + a, b_ref[...] + b
        a_ref[...], b_ref[...] = a, b
    at_ref[...], bt_ref[...] = a_ref[...].T, b_ref[...].T


def pre(pieces, token, w_gate, w_up):
    width, columns = w_gate.shape
    tokens = sum(p.shape[0] for p in pieces)
    count = len(pieces)
    return kernel_call(
        functools.partial(pre_kernel, count),
        [*pieces, token, w_gate, w_up],
        [jax.ShapeDtypeStruct((columns, tokens), F32)] * 2
        + [jax.ShapeDtypeStruct((width, tokens), BF16), jax.ShapeDtypeStruct((8, LANES), F32)],
        6,
        4 * tokens * width * columns,
        2 * tokens * width,
        scratch_shapes=[pltpu.VMEM((tokens, columns), F32)] * 2,
    )


def core_kernel(count, experts, split, *refs):
    pieces, refs = refs[:count], refs[count:]
    at_ref, bt_ref, down_ref, gate_ref, up_ref = refs[:5]
    c_ref, ggt_ref, ugt_ref, ht_ref, near_ref, far_ref = refs[5:11]
    downs, gate_slots, up_slots, down_sems, gate_sems, up_sems = refs[11:]
    columns, width = down_ref.shape
    each, block, depth = columns // experts, downs.shape[1], gate_slots.shape[1]
    steps, turns, half = columns // block, width // depth, near_ref.shape[0]
    ahead = STREAM - 1

    def arrivals(ref, slots, sems, step):
        rows = pl.ds(pl.multiple_of(step * slots.shape[1], slots.shape[1]), slots.shape[1])
        slot = lax.rem(step, STREAM)
        return pltpu.make_async_copy(ref.at[rows], slots.at[slot], sems.at[slot])

    def down(step):
        return arrivals(down_ref, downs, down_sems, step)

    def gate(turn):
        return arrivals(gate_ref, gate_slots, gate_sems, turn)

    def up(turn):
        return arrivals(up_ref, up_slots, up_sems, turn)

    def start_pair(turn):
        gate(turn).start()
        up(turn).start()

    for step in range(min(ahead, steps)):
        down(jnp.int32(step)).start()
    for turn in range(min(ahead, turns) - min(ahead, steps)):
        start_pair(jnp.int32(turn))
    at = 0
    for piece in pieces:
        c_ref[pl.ds(at, piece.shape[0]), :] = piece[:, :width]
        at += piece.shape[0]
    gates = joined(pieces, slice(width, None)).astype(F32).T
    line = lax.broadcasted_iota(jnp.int32, gates.shape, 0)
    first = lax.axis_index("expert") * experts // split
    begun = max(0, min(ahead, turns) - min(ahead, steps))

    def units(step, carry):
        down(step).wait()
        last = step + ahead - steps

        @pl.when(last < 0)
        def _():
            down(step + ahead).start()

        @pl.when((last >= begun) & (last < min(ahead, turns)))
        def _():
            start_pair(last)

        rows = pl.ds(pl.multiple_of(step * block, block), block)
        own = line == first + step * block // each
        weight = jnp.sum(jnp.where(own, gates, 0.0), axis=0, keepdims=True)
        hidden_grad = weight * contract(downs[lax.rem(step, STREAM)], c_ref[...], 1, 1)
        a, b = at_ref[rows, :], bt_ref[rows, :]
        g = jax.nn.sigmoid(a)
        active = a * g
        ht_ref[rows, :] = (weight * (active * b)).astype(BF16)
        ugt_ref[rows, :] = (hidden_grad * active).astype(BF16)
        ggt_ref[rows, :] = (hidden_grad * b * g * (1.0 + a * (1.0 - g))).astype(BF16)
        return carry

    def rows_out(turn, carry):
        gate(turn).wait()
        up(turn).wait()

        @pl.when(turn + ahead < turns)
        def _():
            start_pair(turn + ahead)

        rows, slot = pl.ds(pl.multiple_of(turn * depth, depth), depth), lax.rem(turn, STREAM)
        total = jnp.dot(gate_slots[slot], ggt_ref[...], preferred_element_type=F32)
        total += jnp.dot(up_slots[slot], ugt_ref[...], preferred_element_type=F32)
        total = total.T.astype(BF16)
        near_ref[:, rows] = total[:half]
        far_ref[:, rows] = total[half:]
        return carry

    lax.fori_loop(0, steps, units, 0)
    lax.fori_loop(0, turns, rows_out, 0)


def core(pieces, at, bt, w_down, w_gate, w_up, experts, split):
    columns, width = w_down.shape
    tokens = at.shape[1]
    block, depth = min(256, columns // experts), min(512, width)
    return kernel_call(
        functools.partial(core_kernel, len(pieces), experts, split),
        [*pieces, at, bt, in_hbm(w_down), in_hbm(w_gate), in_hbm(w_up)],
        [jax.ShapeDtypeStruct((tokens, width), BF16)]
        + [jax.ShapeDtypeStruct((columns, tokens), BF16)] * 3
        + [jax.ShapeDtypeStruct((tokens // 2, width), BF16)] * 2,
        30,
        12 * tokens * width * columns,
        6 * width * columns,
        in_specs=[WHOLE] * (len(pieces) + 2) + [pl.BlockSpec(memory_space=pltpu.HBM)] * 3,
        scratch_shapes=[pltpu.VMEM((STREAM, block, width), BF16)]
        + [pltpu.VMEM((STREAM, depth, columns), BF16)] * 2
        + [pltpu.SemaphoreType.DMA((STREAM,))] * 3,
    )


def grads_kernel(form, *refs):
    count = len(form)
    operands, outs = refs[: 2 * count], refs[2 * count + 1 : 3 * count + 1]
    token_ref, slots, sems = refs[3 * count + 1 :]
    token_ref[...] = refs[2 * count][...]
    flying, turn = {}, 0
    for k, right_dim in enumerate(form):
        left, right, out = operands[2 * k], operands[2 * k + 1], outs[k]
        rows, columns = out.shape
        wide = slots.shape[2]
        block = slots.shape[1] * wide // columns
        for start in range(0, rows, slots.shape[1]):
            at = pl.ds(start, slots.shape[1])
            for side in range(0, columns, wide):
                slot = turn % SLOTS
                turn += 1
                if slot in flying:
                    flying.pop(slot).wait()
                part = pl.ds(side, wide)
                rhs = right[:, part] if right_dim == 0 else right[part, :]
                slots[slot] = contract(left[at, :], rhs, 1, right_dim).astype(BF16)
                flying[slot] = pltpu.make_async_copy(slots.at[slot], out.at[at, part], sems.at[slot])
                flying[slot].start()
    for copy in flying.values():
        copy.wait()


def grads(token, *products):
    operands, outs, form, flops = [], [], [], 0
    for left, right, right_dim in products:
        operands += [left, right]
        form.append(right_dim)
        outs.append(jax.ShapeDtypeStruct((left.shape[0], right.shape[1 - right_dim]), BF16))
        flops += 4 * left.size * right.shape[1 - right_dim]
    wide = min(2048, min(o.shape[1] for o in outs))
    high = min(512, min(o.shape[0] for o in outs))
    moved = sum(2 * o.size for o in outs)
    return kernel_call(
        functools.partial(grads_kernel, tuple(form)),
        [*operands, token],
        [*outs, jax.ShapeDtypeStruct(token.shape, token.dtype)],
        20,
        flops,
        moved,
        out_specs=[pl.BlockSpec(memory_space=pltpu.HBM)] * len(outs) + [WHOLE],
        scratch_shapes=[pltpu.VMEM((SLOTS, high, wide), BF16), pltpu.SemaphoreType.DMA((SLOTS,))],
    )


def hand_on(mine, mask):
    devices, sections = lax.axis_size("expert"), lax.axis_size("section")
    route = [
        (s * devices + i, (s - 1) % sections * devices + (i ^ (2 * mask)))
        for s in range(sections)
        for i in range(devices)
    ]
    return lax.ppermute(mine, ("section", "expert"), route)


def body(layer_input, w_gate, w_up, w_down, grad_out, expert_ids, gates):
    devices = lax.axis_size("expert")
    experts = max(1, EXPERTS // devices)
    split = max(1, devices // EXPERTS)
    w_gate, w_up, w_down = w_gate[0], w_up[0], w_down[0]
    message, token = message_of(grad_out[0], expert_ids[0], gates[0], 4096 * w_gate.size)
    inputs, token, _ = gather(layer_input[0], token, None)
    inputs = [jnp.concatenate(inputs)] if devices > 8 else inputs
    at, bt, xt, token = pre(inputs, token, w_gate, w_up)
    cotangents, _, token = gather(message, None, token)
    cotangents = [jnp.concatenate(cotangents)] if devices > 8 else cotangents
    c, ggt, ugt, ht, near, far = core(cotangents, at, bt, w_down, w_gate, w_up, experts, split)
    gate_grad, token = grads(token, (xt, ggt, 1))
    mine = (near.astype(F32) + swap(far, 1).astype(F32)).astype(BF16)
    chips = devices // 2
    mine = jnp.split(mine, chips)
    far_first = sorted(range(chips), reverse=True)
    early = [m for m in far_first if m >= chips - chips // 4 or m < chips // 4]
    late = [m for m in far_first if m not in early]
    mine, token = lax.optimization_barrier((mine, token))
    arrived = [hand_on(mine[m], m) for m in early]
    up_grad, token = grads(token, (xt, ugt, 1))
    mine, token = lax.optimization_barrier((mine, token))
    arrived += [hand_on(mine[m], m) for m in late]
    down_grad, _ = grads(token, (ht, c, 0))
    grad_prev = functools.reduce(jnp.add, [part.astype(F32) for part in arrived]).astype(BF16)
    return grad_prev[None], gate_grad[None], up_grad[None], down_grad[None]


def solution(mesh):
    tokens, columns = P("section", "expert", None), P("section", None, "expert")
    return jax.shard_map(
        body,
        mesh=mesh,
        in_specs=(tokens, columns, columns, tokens, tokens, tokens, tokens),
        out_specs=(tokens, columns, columns, tokens),
        check_vma=False,
    )
```

```python
import functools

import jax
import jax.numpy as jnp
from jax import lax
from jax.experimental import pallas as pl
from jax.experimental.pallas import tpu as pltpu
from jax.sharding import PartitionSpec as P

EXPERTS = 16
LANES = 128
SLOTS = 4
STREAM = 4
BF16, F32 = jnp.bfloat16, jnp.float32
MIB = 1 << 20
WHOLE = pl.BlockSpec(memory_space=pltpu.VMEM)


def contract(left, right, left_dim, right_dim):
    return lax.dot_general(
        left, right, (((left_dim,), (right_dim,)), ((), ())), preferred_element_type=F32
    )


def swap(block, bits):
    devices = lax.axis_size("expert")
    return lax.ppermute(block, "expert", [(i, i ^ bits) for i in range(devices)])


def gather(block, ahead, after):
    near = {0: block}
    chips = lax.axis_size("expert") // 2
    bits = chips
    while bits > 1:
        near |= {mask | bits: swap(part, bits) for mask, part in near.items()}
        if ahead is not None and bits == chips:
            near[bits], ahead = lax.optimization_barrier((near[bits], ahead))
        bits //= 2
    parts = [near[mask] for mask in sorted(near)]
    other = [swap(part, 1) for part in parts[:-1]]
    if after is not None:
        parts[-1], after = lax.optimization_barrier((parts[-1], after))
    return parts + other + [swap(parts[-1], 1)], ahead, after


def in_hbm(array):
    return pltpu.with_memory_space_constraint(array, pltpu.HBM)


def kernel_call(kernel, operands, outs, limit, flops, moved, **more):
    specs = more.pop("in_specs", [WHOLE] * len(operands))
    return pl.pallas_call(
        kernel,
        in_specs=specs,
        out_specs=more.pop("out_specs", [WHOLE] * len(outs)),
        out_shape=outs,
        compiler_params=pltpu.CompilerParams(vmem_limit_bytes=limit * MIB),
        cost_estimate=pl.CostEstimate(flops=flops, bytes_accessed=moved, transcendentals=0),
        **more,
    )(*operands)


def joined(refs, columns):
    parts = [r[:, columns] for r in refs]
    return jnp.concatenate(parts, axis=0) if len(parts) > 1 else parts[0]


def message_kernel(grad_ref, ids_ref, gates_ref, out_ref, token_ref):
    token_ref[...] = jnp.zeros_like(token_ref)
    rows, width = grad_ref.shape
    out_ref[:, :width] = grad_ref[...]
    lane = lax.broadcasted_iota(jnp.int32, (rows, LANES), 1)
    weight = jnp.zeros((rows, LANES), F32)
    for k in range(ids_ref.shape[1]):
        own = ids_ref[:, k : k + 1] == lane
        weight += jnp.where(own, gates_ref[:, k : k + 1].astype(F32), 0.0)
    out_ref[:, width:] = weight.astype(BF16)


def message_of(grad_out, ids, gates, beside):
    rows, width = grad_out.shape
    return kernel_call(
        message_kernel,
        [grad_out, ids, gates],
        [jax.ShapeDtypeStruct((rows, width + LANES), BF16), jax.ShapeDtypeStruct((8, LANES), F32)],
        4,
        beside,
        4 * rows * width,
    )


def pre_kernel(count, *refs):
    pieces, refs = refs[:count], refs[count + 1 :]
    gate_ref, up_ref, at_ref, bt_ref, xt_ref, token_ref, a_ref, b_ref = refs
    token_ref[...] = jnp.zeros_like(token_ref)
    width = gate_ref.shape[0]
    depth = min(512, width)
    for start in range(0, width, depth):
        rows = pl.ds(start, depth)
        x = joined(pieces, rows)
        xt_ref[rows, :] = x.T
        a = jnp.dot(x, gate_ref[rows, :], preferred_element_type=F32)
        b = jnp.dot(x, up_ref[rows, :], preferred_element_type=F32)
        if start:
            a, b = a_ref[...] + a, b_ref[...] + b
        a_ref[...], b_ref[...] = a, b
    at_ref[...], bt_ref[...] = a_ref[...].T, b_ref[...].T


def pre(pieces, token, w_gate, w_up):
    width, columns = w_gate.shape
    tokens = sum(p.shape[0] for p in pieces)
    count = len(pieces)
    return kernel_call(
        functools.partial(pre_kernel, count),
        [*pieces, token, w_gate, w_up],
        [jax.ShapeDtypeStruct((columns, tokens), F32)] * 2
        + [jax.ShapeDtypeStruct((width, tokens), BF16), jax.ShapeDtypeStruct((8, LANES), F32)],
        6,
        4 * tokens * width * columns,
        2 * tokens * width,
        scratch_shapes=[pltpu.VMEM((tokens, columns), F32)] * 2,
    )


def core_kernel(count, experts, split, *refs):
    pieces, refs = refs[:count], refs[count:]
    at_ref, bt_ref, down_ref, gate_ref, up_ref = refs[:5]
    c_ref, ggt_ref, ugt_ref, ht_ref, near_ref, far_ref = refs[5:11]
    downs, gate_slots, up_slots, down_sems, gate_sems, up_sems = refs[11:]
    columns, width = down_ref.shape
    each, block, depth = columns // experts, downs.shape[1], gate_slots.shape[1]
    steps, turns, half = columns // block, width // depth, near_ref.shape[0]
    ahead = STREAM - 1

    def arrivals(ref, slots, sems, step):
        rows = pl.ds(pl.multiple_of(step * slots.shape[1], slots.shape[1]), slots.shape[1])
        slot = lax.rem(step, STREAM)
        return pltpu.make_async_copy(ref.at[rows], slots.at[slot], sems.at[slot])

    def down(step):
        return arrivals(down_ref, downs, down_sems, step)

    def gate(turn):
        return arrivals(gate_ref, gate_slots, gate_sems, turn)

    def up(turn):
        return arrivals(up_ref, up_slots, up_sems, turn)

    def start_pair(turn):
        gate(turn).start()
        up(turn).start()

    for step in range(min(ahead, steps)):
        down(jnp.int32(step)).start()
    for turn in range(min(ahead, turns) - min(ahead, steps)):
        start_pair(jnp.int32(turn))
    at = 0
    for piece in pieces:
        c_ref[pl.ds(at, piece.shape[0]), :] = piece[:, :width]
        at += piece.shape[0]
    gates = joined(pieces, slice(width, None)).astype(F32).T
    line = lax.broadcasted_iota(jnp.int32, gates.shape, 0)
    first = lax.axis_index("expert") * experts // split
    begun = max(0, min(ahead, turns) - min(ahead, steps))

    def units(step, carry):
        down(step).wait()
        last = step + ahead - steps

        @pl.when(last < 0)
        def _():
            down(step + ahead).start()

        @pl.when((last >= begun) & (last < min(ahead, turns)))
        def _():
            start_pair(last)

        rows = pl.ds(pl.multiple_of(step * block, block), block)
        own = line == first + step * block // each
        weight = jnp.sum(jnp.where(own, gates, 0.0), axis=0, keepdims=True)
        hidden_grad = weight * contract(downs[lax.rem(step, STREAM)], c_ref[...], 1, 1)
        a, b = at_ref[rows, :], bt_ref[rows, :]
        g = jax.nn.sigmoid(a)
        active = a * g
        ht_ref[rows, :] = (weight * (active * b)).astype(BF16)
        ugt_ref[rows, :] = (hidden_grad * active).astype(BF16)
        ggt_ref[rows, :] = (hidden_grad * b * g * (1.0 + a * (1.0 - g))).astype(BF16)
        return carry

    def rows_out(turn, carry):
        gate(turn).wait()
        up(turn).wait()

        @pl.when(turn + ahead < turns)
        def _():
            start_pair(turn + ahead)

        rows, slot = pl.ds(pl.multiple_of(turn * depth, depth), depth), lax.rem(turn, STREAM)
        total = jnp.dot(gate_slots[slot], ggt_ref[...], preferred_element_type=F32)
        total += jnp.dot(up_slots[slot], ugt_ref[...], preferred_element_type=F32)
        total = total.T.astype(BF16)
        near_ref[:, rows] = total[:half]
        far_ref[:, rows] = total[half:]
        return carry

    lax.fori_loop(0, steps, units, 0)
    lax.fori_loop(0, turns, rows_out, 0)


def core(pieces, at, bt, w_down, w_gate, w_up, experts, split):
    columns, width = w_down.shape
    tokens = at.shape[1]
    block, depth = min(256, columns // experts), min(512, width)
    return kernel_call(
        functools.partial(core_kernel, len(pieces), experts, split),
        [*pieces, at, bt, in_hbm(w_down), in_hbm(w_gate), in_hbm(w_up)],
        [jax.ShapeDtypeStruct((tokens, width), BF16)]
        + [jax.ShapeDtypeStruct((columns, tokens), BF16)] * 3
        + [jax.ShapeDtypeStruct((tokens // 2, width), BF16)] * 2,
        30,
        12 * tokens * width * columns,
        6 * width * columns,
        in_specs=[WHOLE] * (len(pieces) + 2) + [pl.BlockSpec(memory_space=pltpu.HBM)] * 3,
        scratch_shapes=[pltpu.VMEM((STREAM, block, width), BF16)]
        + [pltpu.VMEM((STREAM, depth, columns), BF16)] * 2
        + [pltpu.SemaphoreType.DMA((STREAM,))] * 3,
    )


def grads_kernel(form, *refs):
    count = len(form)
    operands, outs = refs[: 2 * count], refs[2 * count + 1 : 3 * count + 1]
    token_ref, slots, sems = refs[3 * count + 1 :]
    token_ref[...] = refs[2 * count][...]
    flying, turn = {}, 0
    for k, right_dim in enumerate(form):
        left, right, out = operands[2 * k], operands[2 * k + 1], outs[k]
        rows, columns = out.shape
        wide = slots.shape[2]
        block = slots.shape[1] * wide // columns
        for start in range(0, rows, slots.shape[1]):
            at = pl.ds(start, slots.shape[1])
            for side in range(0, columns, wide):
                slot = turn % SLOTS
                turn += 1
                if slot in flying:
                    flying.pop(slot).wait()
                part = pl.ds(side, wide)
                rhs = right[:, part] if right_dim == 0 else right[part, :]
                slots[slot] = contract(left[at, :], rhs, 1, right_dim).astype(BF16)
                flying[slot] = pltpu.make_async_copy(slots.at[slot], out.at[at, part], sems.at[slot])
                flying[slot].start()
    for copy in flying.values():
        copy.wait()


def grads(token, *products):
    operands, outs, form, flops = [], [], [], 0
    for left, right, right_dim in products:
        operands += [left, right]
        form.append(right_dim)
        outs.append(jax.ShapeDtypeStruct((left.shape[0], right.shape[1 - right_dim]), BF16))
        flops += 4 * left.size * right.shape[1 - right_dim]
    wide = min(2048, min(o.shape[1] for o in outs))
    high = min(512, min(o.shape[0] for o in outs))
    moved = sum(2 * o.size for o in outs)
    return kernel_call(
        functools.partial(grads_kernel, tuple(form)),
        [*operands, token],
        [*outs, jax.ShapeDtypeStruct(token.shape, token.dtype)],
        20,
        flops,
        moved,
        out_specs=[pl.BlockSpec(memory_space=pltpu.HBM)] * len(outs) + [WHOLE],
        scratch_shapes=[pltpu.VMEM((SLOTS, high, wide), BF16), pltpu.SemaphoreType.DMA((SLOTS,))],
    )


def hand_on(mine, mask):
    devices, sections = lax.axis_size("expert"), lax.axis_size("section")
    route = [
        (s * devices + i, (s - 1) % sections * devices + (i ^ (2 * mask)))
        for s in range(sections)
        for i in range(devices)
    ]
    return lax.ppermute(mine, ("section", "expert"), route)


def body(layer_input, w_gate, w_up, w_down, grad_out, expert_ids, gates):
    devices = lax.axis_size("expert")
    experts = max(1, EXPERTS // devices)
    split = max(1, devices // EXPERTS)
    w_gate, w_up, w_down = w_gate[0], w_up[0], w_down[0]
    message, token = message_of(grad_out[0], expert_ids[0], gates[0], 4096 * w_gate.size)
    inputs, token, _ = gather(layer_input[0], token, None)
    inputs = [jnp.concatenate(inputs)] if devices > 8 else inputs
    at, bt, xt, token = pre(inputs, token, w_gate, w_up)
    cotangents, _, token = gather(message, None, token)
    cotangents = [jnp.concatenate(cotangents)] if devices > 8 else cotangents
    c, ggt, ugt, ht, near, far = core(cotangents, at, bt, w_down, w_gate, w_up, experts, split)
    gate_grad, token = grads(token, (xt, ggt, 1))
    mine = (near.astype(F32) + swap(far, 1).astype(F32)).astype(BF16)
    chips = devices // 2
    mine = jnp.split(mine, chips)
    far_first = sorted(range(chips), reverse=True)
    mine, token = lax.optimization_barrier((mine, token))
    arrived = [hand_on(mine[m], m) for m in far_first]
    up_grad, down_grad, _ = grads(token, (xt, ugt, 1), (ht, c, 0))
    grad_prev = functools.reduce(jnp.add, [part.astype(F32) for part in arrived]).astype(BF16)
    return grad_prev[None], gate_grad[None], up_grad[None], down_grad[None]


def solution(mesh):
    tokens, columns = P("section", "expert", None), P("section", None, "expert")
    return jax.shard_map(
        body,
        mesh=mesh,
        in_specs=(tokens, columns, columns, tokens, tokens, tokens, tokens),
        out_specs=(tokens, columns, columns, tokens),
        check_vma=False,
    )
```
